32 devices in a mesh: dom: 4 (over z), shard: 8 (over y, x, core).
Axes of the slice: x: 2, y: 2, z: 4, core: 2. Of those that a mesh axis runs over, the one named last changes fastest.
Arguments:
- embedding: float32 [4096, 400], P(('dom', 'shard')), may hold values from -0.9 to 0.9
- accumulator: float32 [4096], P(('dom', 'shard')), may hold values from 0.1 to 1
- relation: float32 [16, 400], replicated, may hold values from 0.1 to 1.9
- plan: int32 [4], replicated, may hold values from 0 to 3, as said below
- lhs_index: int32 [49152], P(('dom', 'shard')), may hold values from 0 to 127
- rhs_index: int32 [49152], P(('dom', 'shard')), may hold values from 0 to 127
- rel_index: int32 [49152], P(('dom', 'shard')), may hold values from 0 to 15
- slot_count: int32 [32, 8], P(('dom', 'shard')), may hold values from 1 to 192, as said below
- neg_span: int32 [96], P(('dom', 'shard')), may hold values from 0 to 2
Outputs:
- entity_grad: float32 [4096, 400], P(('dom', 'shard'))
- adagrad_state: float32 [4096], P(('dom', 'shard'))
- relation_grad: float32 [16, 400], replicated
The draws below stay inside these ranges and needn't reach their ends.
Inputs may be any that keep to these rules, and one draw needn't show every extreme that they name: plan[d] = d XOR m for one m of 1 to 4 - 1, the same for all d. `slot_count`: every row of groups has some full slot.
All inputs are finite; a program needn't handle non-finite values.
Results may differ from the reference program's by a relative error of at most 0.00079.
Values sent between devices are 32-bit elements; how exact they have to be, the bound alone decides.
A program may use at most 64 MiB of HBM per device.

```python
import math
import jax
import jax.numpy as jnp
from jax import lax

W = 400
NREL = 16
R = 128
E = 1536
CH = 512
SLOT = 192
SPANS = 3
ROWS = 4096
EDGES = 49152
N_DOM = 4
N_SHARD = 8


def draw_embedding(key, part):
    key = jax.random.fold_in(key, 11)
    base_key = jax.random.fold_in(key, 0)
    values = jnp.clip(0.15 * jax.random.normal(base_key, (ROWS, W), jnp.float32), -0.9, 0.9)
    return values.astype(jnp.float32)


def draw_plan(key, part):
    key = jax.random.fold_in(key, 23)
    flip_mask = jax.random.randint(key, (), 1, N_DOM, dtype=jnp.int32)
    return jnp.bitwise_xor(jnp.arange(N_DOM, dtype=jnp.int32), flip_mask).astype(jnp.int32)


def draw_slot_count(key, part):
    key = jax.random.fold_in(key, 37)
    count_key, full_key, shared_key, single_key = jax.random.split(key, 4)
    lowest = max(SLOT // 4, 1)
    counts = jax.random.randint(count_key, (N_DOM * N_SHARD, N_SHARD), lowest, SLOT + 1, dtype=jnp.int32)
    full_slot = jax.random.randint(full_key, (N_DOM * N_SHARD, 1), 0, N_SHARD, dtype=jnp.int32)
    shared_slot = jax.random.randint(shared_key, (), 0, N_SHARD, dtype=jnp.int32)
    single_row = jax.random.randint(single_key, (), 0, N_DOM * N_SHARD, dtype=jnp.int32)
    columns = jnp.arange(N_SHARD, dtype=jnp.int32)[None, :]
    rows_seen = jnp.arange(N_DOM * N_SHARD, dtype=jnp.int32)[:, None]
    counts = jnp.where(columns == full_slot, SLOT, counts)
    counts = jnp.where(columns == shared_slot, SLOT, counts)
    single_col = (shared_slot + 1) % N_SHARD
    counts = jnp.where((rows_seen == single_row) & (columns == single_col), 1, counts)
    return counts.astype(jnp.int32)


def with_ends(drawn, rng, smallest, top_value):
    spot = [jax.random.randint(jax.random.fold_in(rng, axis), (), 0, length) for axis, length in enumerate(drawn.shape)]
    widest = drawn.shape.index(max(drawn.shape))
    beside = spot[:widest] + [(spot[widest] + 1) % drawn.shape[widest]] + spot[widest + 1:]
    return drawn.at[tuple(spot)].set(smallest).at[tuple(beside)].set(top_value)


def shard_levels(own_key, shape, cuts, smallest, high):
    loudness = 1.0
    for axis_at, shards_of in cuts:
        heights = jax.random.uniform(jax.random.fold_in(jax.random.fold_in(own_key, 6), axis_at), (shards_of,), jnp.float32, smallest / len(cuts), high / len(cuts))
        loudness = loudness * jnp.repeat(jnp.exp(heights), shape[axis_at] // shards_of).reshape((-1,) + (1,) * (len(shape) - 1 - axis_at))
    return loudness


def setup_inputs(seed: int = 0) -> dict:
    splits = jax.random.split(jax.random.key(seed), 10)
    embedding = draw_embedding(jax.random.fold_in(splits[9], 71), 0)
    accumulator = jnp.clip(jnp.exp(math.log(1.0) - 2.3025851 * jax.random.uniform(splits[1], (ROWS,), jnp.float32) ** shard_levels(splits[1], (ROWS,), ((0, 32),), -0.2, 0.2)), 0.1, 1.0)
    relation = jnp.clip(1.0 + 0.18 * jax.random.normal(splits[2], (NREL, W), jnp.float32), 0.1, 1.9)
    plan = draw_plan(jax.random.fold_in(splits[9], 71), 0)
    lhs_index = with_ends(jax.random.randint(splits[4], (EDGES,), 0, R), jax.random.fold_in(splits[4], 1), 0, R - 1).astype(jnp.int32)
    rhs_index = with_ends(jax.random.randint(splits[5], (EDGES,), 0, R), jax.random.fold_in(splits[5], 1), 0, R - 1).astype(jnp.int32)
    rel_index = with_ends(jax.random.randint(splits[6], (EDGES,), 0, NREL), jax.random.fold_in(splits[6], 1), 0, NREL - 1).astype(jnp.int32)
    slot_count = draw_slot_count(jax.random.fold_in(splits[9], 71), 0)
    neg_span = with_ends(jax.random.randint(splits[8], (N_DOM * N_SHARD * SPANS,), 0, SPANS), jax.random.fold_in(splits[8], 1), 0, SPANS - 1).astype(jnp.int32)
    return {"embedding": embedding, "accumulator": accumulator, "relation": relation, "plan": plan, "lhs_index": lhs_index, "rhs_index": rhs_index, "rel_index": rel_index, "slot_count": slot_count, "neg_span": neg_span}


def soft_weights(positive, scores, live_cols):
    masked = jnp.where(live_cols, scores, -jnp.inf)
    row_max = jnp.maximum(positive, jnp.max(masked, axis=1))
    own_term = jnp.exp(positive - row_max)
    others = jnp.exp(masked - row_max[:, None])
    summed = own_term + jnp.sum(others, axis=1)
    return others / summed[:, None], own_term / summed


def add_rows(values, first_row, update):
    current = lax.dynamic_slice_in_dim(values, first_row, update.shape[0], 0)
    return lax.dynamic_update_slice_in_dim(values, current + update, first_row, 0)


def edge_grads(lhs_rows, rel_rows, rhs_rows, valid_rows, negatives, block_size):
    block_count = lhs_rows.shape[0] // block_size
    inner = (((1,), (1,)), ((), ()))
    outer = (((0,), (0,)), ((), ()))

    def one_block(block_index, grad_parts):
        grad_lhs, grad_rhs, grad_rel = grad_parts
        first_row = (block_index * block_size).astype(jnp.int32)
        neg_first = (negatives[block_index] * block_size).astype(jnp.int32)
        lhs_here = lax.dynamic_slice_in_dim(lhs_rows, first_row, block_size, 0)
        rhs_here = lax.dynamic_slice_in_dim(rhs_rows, first_row, block_size, 0)
        rel_here = lax.dynamic_slice_in_dim(rel_rows, first_row, block_size, 0)
        live_here = lax.dynamic_slice_in_dim(valid_rows, first_row, block_size, 0)
        lhs_neg = lax.dynamic_slice_in_dim(lhs_rows, neg_first, block_size, 0).astype(jnp.bfloat16)
        rhs_neg = lax.dynamic_slice_in_dim(rhs_rows, neg_first, block_size, 0).astype(jnp.bfloat16)
        live_neg = lax.dynamic_slice_in_dim(valid_rows, neg_first, block_size, 0)
        left = lhs_here * rel_here
        right = rhs_here * rel_here
        positive = jnp.sum(left * rhs_here, axis=1)
        left_b = left.astype(jnp.bfloat16)
        right_b = right.astype(jnp.bfloat16)
        tail_scores = lax.dot_general(left_b, rhs_neg, inner, preferred_element_type=jnp.float32)
        head_scores = lax.dot_general(right_b, lhs_neg, inner, preferred_element_type=jnp.float32)
        live_cols = live_neg[None, :] > 0.5
        tail_prob, tail_pos = soft_weights(positive, tail_scores, live_cols)
        head_prob, head_pos = soft_weights(positive, head_scores, live_cols)
        weight_pos = live_here * (tail_pos + head_pos - 2.0)
        tail_w = (live_here[:, None] * tail_prob).astype(jnp.bfloat16)
        head_w = (live_here[:, None] * head_prob).astype(jnp.bfloat16)
        grad_left = weight_pos[:, None] * rhs_here + jnp.dot(tail_w, rhs_neg, preferred_element_type=jnp.float32)
        grad_right = jnp.dot(head_w, lhs_neg, preferred_element_type=jnp.float32)
        grad_lhs = add_rows(grad_lhs, first_row, grad_left * rel_here)
        grad_rhs = add_rows(grad_rhs, first_row, weight_pos[:, None] * left + grad_right * rel_here)
        grad_rel = add_rows(grad_rel, first_row, grad_left * lhs_here + grad_right * rhs_here)
        grad_rhs = add_rows(grad_rhs, neg_first, lax.dot_general(tail_w, left_b, outer, preferred_element_type=jnp.float32))
        grad_lhs = add_rows(grad_lhs, neg_first, lax.dot_general(head_w, right_b, outer, preferred_element_type=jnp.float32))
        return (grad_lhs, grad_rhs, grad_rel)

    empty_grad = jnp.zeros_like(lhs_rows)
    return lax.fori_loop(0, block_count, one_block, (empty_grad, empty_grad, empty_grad))


def reference(embedding, accumulator, relation, plan, lhs_index, rhs_index, rel_index, slot_count, neg_span):
    group_count = N_DOM * N_SHARD
    lhs_groups = lhs_index.reshape(group_count, E)
    rhs_groups = rhs_index.reshape(group_count, E)
    rel_groups = rel_index.reshape(group_count, E)
    neg_groups = neg_span.reshape(group_count, SPANS)

    def one_group(running, inputs):
        table_grad, rel_grad = running
        group, lhs_local, rhs_local, rel_local, counts, negatives = inputs
        dom_index = group // N_SHARD
        partner = plan[dom_index]
        owner_shard = jnp.arange(E, dtype=jnp.int32) // SLOT
        lhs_global = (group * R + lhs_local).astype(jnp.int32)
        rhs_global = ((partner * N_SHARD + owner_shard) * R + rhs_local).astype(jnp.int32)
        valid_rows = (jnp.arange(SLOT, dtype=jnp.int32)[None, :] < counts[:, None]).reshape(E).astype(embedding.dtype)
        lhs_rows = embedding[lhs_global]
        rhs_rows = embedding[rhs_global]
        rel_rows = relation[rel_local]
        grad_lhs, grad_rhs, grad_rel = edge_grads(lhs_rows, rel_rows, rhs_rows, valid_rows, negatives, CH)
        table_grad = table_grad.at[lhs_global].add(grad_lhs).at[rhs_global].add(grad_rhs)
        rel_grad = rel_grad.at[rel_local].add(grad_rel)
        return (table_grad, rel_grad), None

    groups = jnp.arange(group_count, dtype=jnp.int32)
    start_state = (jnp.zeros_like(embedding), jnp.zeros_like(relation))
    (table_grad, rel_grad), _ = lax.scan(one_group, start_state, (groups, lhs_groups, rhs_groups, rel_groups, slot_count, neg_groups))
    adagrad_state = accumulator + jnp.mean(table_grad * table_grad, axis=1)
    return (table_grad, adagrad_state, rel_grad)
```

```python
import functools
import math

import jax
import jax.numpy as jnp
from jax import lax
from jax.experimental import pallas as pl
from jax.experimental.pallas import tpu as pltpu
from jax.sharding import PartitionSpec as P

CH = 512
LANES = 128
MESH = pl.DeviceIdType.MESH
TN = (((0,), (0,)), ((), ()))
NT = (((1,), (1,)), ((), ()))
F32 = jnp.float32
BF16 = jnp.bfloat16


def flip(index, mask):
    out = index
    bit = 1
    while bit <= mask:
        if mask & bit:
            out = out + bit * (1 - 2 * lax.rem(index // bit, 2))
        bit *= 2
    return out


def greet(peers):
    barrier = pltpu.get_barrier_semaphore()
    for peer in peers:
        pl.semaphore_signal(barrier, inc=1, device_id=peer, device_id_type=MESH)
    pl.semaphore_wait(barrier, len(peers))


def send(src, dst, send_sem, recv_sem, peer):
    copy = pltpu.make_async_remote_copy(
        src_ref=src, dst_ref=dst, send_sem=send_sem, recv_sem=recv_sem, device_id=peer, device_id_type=MESH
    )
    copy.start()
    return copy


def fetch_kernel(mask, shards, emb, pack, lhs_out, pack_out, table, own_sem, pair_s, pair_r, chip_s, chip_r, sib_s, sib_r):
    chips = shards // 2
    dom, me = lax.axis_index("dom"), lax.axis_index("shard")
    chip, core = me // 2, lax.rem(me, 2)
    sibling = {"shard": chip * 2 + 1 - core}
    pair = {"dom": flip(dom, mask)}
    others = [{"shard": lax.rem(chip + j, chips) * 2 + core} for j in range(1, chips)]
    own = pltpu.make_async_copy(emb, table.at[me], own_sem)
    own.start()
    greet([sibling, pair] + others)
    moves = [
        send(pack, pack_out, pair_s.at[0], pair_r.at[0], pair),
        send(emb, lhs_out, pair_s.at[1], pair_r.at[1], pair),
    ]
    direct = [send(emb, table.at[me], chip_s.at[j], chip_r.at[j], others[j]) for j in range(chips - 1)]
    moves.append(send(emb, table.at[me], sib_s.at[chips - 1], sib_r.at[chips - 1], sibling))
    for j in range(chips - 1):
        direct[j].wait_recv()
        block = lax.rem(chip + chips - 1 - j, chips) * 2 + core
        moves.append(send(table.at[block], table.at[block], sib_s.at[j], sib_r.at[j], sibling))
    for copy in direct:
        copy.wait_send()
    for copy in moves:
        copy.wait()
    own.wait()


def split(x):
    high = x.astype(BF16)
    return high, (x - high.astype(F32)).astype(BF16)


def dot2(onehot, parts, dims):
    high = lax.dot_general(onehot, parts[0], dims, preferred_element_type=F32)
    return high + lax.dot_general(onehot, parts[1], dims, preferred_element_type=F32)


def edge_kernel(
    shards, slot, meta, pack, lhs_tab, rhs_tab, relation, drhs, dlhs, drel,
    oh_l, oh_r, oh_rel, lhs_s, rhs_s, lhs_b, rhs_b, glhs, grhs, live_col, live_row,
):
    edges = lhs_s.shape[0]
    rows = lhs_tab.shape[0]
    width = lhs_tab.shape[1]
    rels = relation.shape[0]
    subs = edges // LANES
    runs, run_rows, run = oh_r.shape
    owners = run_rows // rows
    spans = edges // CH

    def onehot(number, count):
        ids = lax.broadcasted_iota(jnp.int32, (count, LANES), 0)
        return jnp.where(ids == number, 1.0, 0.0).astype(BF16)

    lane = lax.broadcasted_iota(jnp.int32, (1, LANES), 1)
    for j in range(subs):
        at = slice(j * LANES, (j + 1) * LANES)
        oh_l[:, at] = onehot(pack[j : j + 1, :], rows)
        oh_rel[:, at] = onehot(pack[2 * subs + j : 2 * subs + j + 1, :], rels)
        place = (j * LANES) % run + lane
        shift = jnp.zeros((1, LANES), jnp.int32)
        for g in range(1, owners):
            shift = shift + jnp.where(place >= g * slot, rows, 0)
        inside = (j * LANES) % run
        oh_r[(j * LANES) // run, :, inside : inside + LANES] = onehot(
            pack[subs + j : subs + j + 1, :] + shift, run_rows
        )
    for o in range(shards):
        steps = lax.broadcasted_iota(jnp.int32, (slot, 1), 0)
        live_col[o * slot : (o + 1) * slot, :] = jnp.where(steps < meta[3 * subs, o], 1.0, 0.0)
    for c in range(spans):
        place = c * CH + lax.broadcasted_iota(jnp.int32, (1, CH), 1)
        live = jnp.zeros((1, CH), F32)
        for o in range(c * CH // slot, min(shards, -(-(c + 1) * CH // slot))):
            here = (place >= o * slot) & (place < o * slot + meta[3 * subs, o])
            live = jnp.where(here, 1.0, live)
        live_row[c] = live

    lhs_parts = split(lhs_tab[...])
    rel_parts = split(relation[...])
    for c in range(spans):
        at = slice(c * CH, (c + 1) * CH)
        high = lax.dot_general(oh_l[:, at], lhs_parts[0], TN, preferred_element_type=F32)
        low = lax.dot_general(oh_l[:, at], lhs_parts[1], TN, preferred_element_type=F32)
        lhs_s[at, :] = high + low
        lhs_b[at, :] = high.astype(BF16)
    for t in range(runs):
        at = slice(t * run, (t + 1) * run)
        parts = split(rhs_tab[t * owners : (t + 1) * owners].reshape(run_rows, width))
        high = lax.dot_general(oh_r[t], parts[0], TN, preferred_element_type=F32)
        low = lax.dot_general(oh_r[t], parts[1], TN, preferred_element_type=F32)
        rhs_s[at, :] = high + low
        rhs_b[at, :] = high.astype(BF16)
    glhs[...] = jnp.zeros_like(glhs)
    grhs[...] = jnp.zeros_like(grhs)
    drel[...] = jnp.zeros_like(drel)

    def soft(positive, scores, cols):
        masked = jnp.where(cols, scores, -jnp.inf)
        top = jnp.maximum(positive, jnp.max(masked, axis=1, keepdims=True))
        own = jnp.exp(positive - top)
        others = jnp.exp(masked - top)
        scale = 1.0 / (own + jnp.sum(others, axis=1, keepdims=True))
        return others, own * scale, scale

    def block(c, carry):
        n = meta[3 * subs + 1, c]
        here = pl.ds(pl.multiple_of(c * CH, CH), CH)
        there = pl.ds(pl.multiple_of(n * CH, CH), CH)
        lhs, rhs = lhs_s[here, :], rhs_s[here, :]
        oh = oh_rel[:, here]
        rel = dot2(oh, rel_parts, TN)
        live = live_col[here, :]
        cols = live_row[n] > 0.5
        left, right = lhs * rel, rhs * rel
        positive = jnp.sum(left * rhs, axis=1, keepdims=True)
        left_b, right_b = left.astype(BF16), right.astype(BF16)
        rhs_neg, lhs_neg = rhs_b[there, :], lhs_b[there, :]
        tail = lax.dot_general(left_b, rhs_neg, NT, preferred_element_type=F32)
        head = lax.dot_general(right_b, lhs_neg, NT, preferred_element_type=F32)
        tail, tail_pos, tail_scale = soft(positive, tail, cols)
        head, head_pos, head_scale = soft(positive, head, cols)
        weight = live * (tail_pos + head_pos - 2.0)
        tail_w = (tail * (live * tail_scale)).astype(BF16)
        head_w = (head * (live * head_scale)).astype(BF16)
        grad_left = weight * rhs + jnp.dot(tail_w, rhs_neg, preferred_element_type=F32)
        grad_right = jnp.dot(head_w, lhs_neg, preferred_element_type=F32)
        glhs[here, :] += grad_left * rel
        grhs[here, :] += weight * left + grad_right * rel
        drel[...] += dot2(oh, split(grad_left * lhs + grad_right * rhs), (((1,), (0,)), ((), ())))
        grhs[there, :] += lax.dot_general(tail_w, left_b, TN, preferred_element_type=F32)
        glhs[there, :] += lax.dot_general(head_w, right_b, TN, preferred_element_type=F32)
        return carry

    lax.fori_loop(0, spans, block, 0)
    plain = (((1,), (0,)), ((), ()))
    dlhs[...] = dot2(oh_l[...], split(glhs[...]), plain)
    for t in range(runs):
        sums = dot2(oh_r[t], split(grhs[t * run : (t + 1) * run, :]), plain)
        drhs[t * owners : (t + 1) * owners] = sums.reshape(owners, rows, width)


def return_kernel(
    mask, doms, shards, drhs, dlhs, drel, accumulator, entity, state, rel_out,
    sib_land, sums, land, pair_land, rel_half, rel_sib, rel_sum, rel_chip, rel_sum2, rel_dom, rel_full, rel_back,
    pair_s, pair_r, sib_s, sib_r, chip_s, chip_r, rsib_s, rsib_r, rchip_s, rchip_r, rdom_s, rdom_r, rback_s, rback_r,
):
    chips = shards // 2
    half = rel_half.shape[0]
    dom, me = lax.axis_index("dom"), lax.axis_index("shard")
    chip, core = me // 2, lax.rem(me, 2)
    sibling = {"shard": chip * 2 + 1 - core}
    pair = {"dom": flip(dom, mask)}
    others = [{"shard": lax.rem(chip + j, chips) * 2 + core} for j in range(1, chips)]
    columns = [{"dom": lax.rem(dom + j, doms)} for j in range(1, doms)]
    greet([sibling] + columns + others)

    mine = pl.ds(pl.multiple_of(core * half, half), half)
    yours = pl.ds(pl.multiple_of((1 - core) * half, half), half)
    rel_half[...] = drel[yours, :]
    moves = [send(rel_half, rel_sib, rsib_s, rsib_r, sibling)]
    siblings = []
    for j in range(chips):
        place = lax.rem(chip + (j + 1) % chips, chips) * 2
        siblings.append(send(drhs.at[place + 1 - core], sib_land.at[j], sib_s.at[j], sib_r.at[j], sibling))
    home = send(dlhs, pair_land, pair_s, pair_r, pair)
    moves[0].wait_recv()
    rel_sum[...] = drel[mine, :] + rel_sib[...]
    rel_moves = [send(rel_sum, rel_chip.at[j], rchip_s.at[j], rchip_r.at[j], others[j]) for j in range(chips - 1)]
    directs = []
    for j in range(chips):
        place = lax.rem(chip + (j + 1) % chips, chips) * 2
        siblings[j].wait_recv()
        sums[j] = drhs[place + core] + sib_land[j]
        if j < chips - 1:
            directs.append(send(sums.at[j], land.at[j], chip_s.at[j], chip_r.at[j], others[j]))
    total = rel_sum[...]
    for j in range(chips - 1):
        rel_moves[j].wait_recv()
        total = total + rel_chip[j]
    rel_sum2[...] = total
    dom_moves = [send(rel_sum2, rel_dom.at[j], rdom_s.at[j], rdom_r.at[j], columns[j]) for j in range(doms - 1)]
    total = rel_sum2[...]
    for j in range(doms - 1):
        dom_moves[j].wait_recv()
    total = jnp.zeros_like(total)
    for d in range(doms):
        j = lax.rem(dom + doms - d, doms)
        total = total + jnp.where(j == 0, rel_sum2[...], rel_dom[jnp.maximum(j - 1, 0)])
    rel_full[...] = total
    back = send(rel_full, rel_back, rback_s, rback_r, sibling)
    grads = sums[chips - 1]
    for j in range(chips - 1):
        directs[j].wait_recv()
        grads = grads + land[j]
    home.wait_recv()
    grads = grads + pair_land[...]
    entity[...] = grads
    squares = lax.dot_general(
        jnp.ones((8, grads.shape[1]), F32), grads * grads, NT, precision=lax.Precision.HIGHEST,
        preferred_element_type=F32,
    )
    state[...] = accumulator[...] + squares[0:1, :] / grads.shape[1]
    back.wait_recv()
    rel_out[mine, :] = total
    rel_out[yours, :] = rel_back[...]
    for copy in moves + siblings + [home, back] + rel_moves + directs + dom_moves:
        copy.wait_send()


def local(doms, shards, embedding, accumulator, relation, plan, lhs_index, rhs_index, rel_index, slot_count, neg_span):
    rows, width = embedding.shape
    rels = relation.shape[0]
    edges = lhs_index.shape[0]
    slot = edges // shards
    chips = shards // 2
    spans = edges // CH
    subs = edges // LANES
    run = math.lcm(slot, LANES)
    runs, owners = edges // run, run // slot
    half = rels // 2
    flips = doms - 1
    any_space = pl.BlockSpec(memory_space=pl.ANY)
    vmem = pl.BlockSpec(memory_space=pltpu.VMEM)
    smem = pl.BlockSpec(memory_space=pltpu.SMEM)
    dma = pltpu.SemaphoreType.DMA
    block = jax.ShapeDtypeStruct((rows, width), F32)
    table_type = jax.ShapeDtypeStruct((shards, rows, width), F32)

    pack_rows = -(-(3 * subs + 2) // 8) * 8
    pad = lambda x, size: jnp.pad(x.reshape(-1), (0, size - x.size))
    pack = jnp.concatenate(
        [lhs_index, rhs_index, rel_index, pad(slot_count, LANES), pad(neg_span, (pack_rows - 3 * subs - 1) * LANES)]
    ).reshape(pack_rows, LANES)
    branch = jnp.clip(plan[0] - 1, 0, flips - 1)

    def fetch(mask, emb, pack):
        return pl.pallas_call(
            functools.partial(fetch_kernel, mask, shards),
            out_shape=(block, jax.ShapeDtypeStruct(pack.shape, jnp.int32), table_type),
            in_specs=[any_space] * 2,
            out_specs=(any_space,) * 3,
            scratch_shapes=[
                dma, dma((2,)), dma((2,)), dma((chips - 1,)), dma((chips - 1,)), dma((chips,)), dma((chips,)),
            ],
            compiler_params=pltpu.CompilerParams(collective_id=mask - 1, has_side_effects=True),
            name="fetch_rows",
        )(emb, pack)

    lhs_tab, edges_in, table = lax.switch(
        branch, [functools.partial(fetch, mask) for mask in range(1, doms)], embedding, pack
    )

    drhs, dlhs, drel = pl.pallas_call(
        functools.partial(edge_kernel, shards, slot),
        out_shape=(table_type, block, jax.ShapeDtypeStruct((rels, width), F32)),
        in_specs=[smem] + [vmem] * 4,
        out_specs=(vmem,) * 3,
        scratch_shapes=[
            pltpu.VMEM((rows, edges), BF16),
            pltpu.VMEM((runs, owners * rows, run), BF16),
            pltpu.VMEM((rels, edges), BF16),
            pltpu.VMEM((edges, width), F32),
            pltpu.VMEM((edges, width), F32),
            pltpu.VMEM((edges, width), BF16),
            pltpu.VMEM((edges, width), BF16),
            pltpu.VMEM((edges, width), F32),
            pltpu.VMEM((edges, width), F32),
            pltpu.VMEM((edges, 1), F32),
            pltpu.VMEM((spans, 1, CH), F32),
        ],
        compiler_params=pltpu.CompilerParams(vmem_limit_bytes=56 * 1024 * 1024),
        name="edge_grads",
    )(edges_in, edges_in, lhs_tab, table, relation)

    def give_back(mask, drhs, dlhs, drel, acc):
        small = pltpu.VMEM((half, width), F32)
        return pl.pallas_call(
            functools.partial(return_kernel, mask, doms, shards),
            out_shape=(
                block,
                jax.ShapeDtypeStruct((1, rows), F32),
                jax.ShapeDtypeStruct((rels, width), F32),
            ),
            in_specs=[vmem] * 4,
            out_specs=(vmem,) * 3,
            scratch_shapes=[
                pltpu.VMEM((chips, rows, width), F32),
                pltpu.VMEM((chips, rows, width), F32),
                pltpu.VMEM((chips - 1, rows, width), F32),
                pltpu.VMEM((rows, width), F32),
                small, small, small,
                pltpu.VMEM((chips - 1, half, width), F32),
                small,
                pltpu.VMEM((doms - 1, half, width), F32),
                small, small,
                dma, dma, dma((chips,)), dma((chips,)), dma((chips - 1,)), dma((chips - 1,)),
                dma, dma, dma((chips - 1,)), dma((chips - 1,)), dma((doms - 1,)), dma((doms - 1,)), dma, dma,
            ],
            compiler_params=pltpu.CompilerParams(
                collective_id=flips + mask - 1, has_side_effects=True, vmem_limit_bytes=56 * 1024 * 1024
            ),
            name="return_grads",
        )(drhs, dlhs, drel, acc)

    entity, state, rel_grad = lax.switch(
        branch,
        [functools.partial(give_back, mask) for mask in range(1, doms)],
        drhs, dlhs, drel, accumulator.reshape(1, rows),
    )
    return entity, state.reshape(rows), rel_grad


def solution(mesh):
    both = ("dom", "shard")
    in_specs = (P(both, None), P(both), P(), P(), P(both), P(both), P(both), P(both, None), P(both))
    out_specs = (P(both, None), P(both), P())
    body = functools.partial(local, mesh.shape["dom"], mesh.shape["shard"])
    return jax.shard_map(body, mesh=mesh, in_specs=in_specs, out_specs=out_specs, check_vma=False)
```

```python
import functools
import math

import jax
import jax.numpy as jnp
from jax import lax
from jax.experimental import pallas as pl
from jax.experimental.pallas import tpu as pltpu
from jax.sharding import PartitionSpec as P

CH = 512
LANES = 128
MESH = pl.DeviceIdType.MESH
TN = (((0,), (0,)), ((), ()))
NT = (((1,), (1,)), ((), ()))
NN = (((1,), (0,)), ((), ()))
F32 = jnp.float32
BF16 = jnp.bfloat16


def flip(index, mask):
    out = index
    bit = 1
    while bit <= mask:
        if mask & bit:
            out = out + bit * (1 - 2 * lax.rem(index // bit, 2))
        bit *= 2
    return out


def greet(peers):
    barrier = pltpu.get_barrier_semaphore()
    for peer in peers:
        pl.semaphore_signal(barrier, inc=1, device_id=peer, device_id_type=MESH)
    pl.semaphore_wait(barrier, len(peers))


def send(src, dst, send_sem, recv_sem, peer):
    copy = pltpu.make_async_remote_copy(
        src_ref=src, dst_ref=dst, send_sem=send_sem, recv_sem=recv_sem, device_id=peer, device_id_type=MESH
    )
    copy.start()
    return copy


def fetch_kernel(mask, shards, *refs):
    emb, edges_in = refs[0], refs[1:6]
    lhs_out, edges_out, table = refs[6], refs[7:12], refs[12]
    own_sem, pair_s, pair_r, chip_s, chip_r, sib_s, sib_r = refs[13:]
    chips = shards // 2
    dom, me = lax.axis_index("dom"), lax.axis_index("shard")
    chip, core = me // 2, lax.rem(me, 2)
    sibling = {"shard": chip * 2 + 1 - core}
    pair = {"dom": flip(dom, mask)}
    others = [{"shard": lax.rem(chip + j, chips) * 2 + core} for j in range(1, chips)]
    own = pltpu.make_async_copy(emb, table.at[me], own_sem)
    own.start()
    greet([sibling, pair] + others)
    moves = [send(emb, lhs_out, pair_s.at[5], pair_r.at[5], pair)]
    direct = [send(emb, table.at[me], chip_s.at[j], chip_r.at[j], others[j]) for j in range(chips - 1)]
    moves.append(send(emb, table.at[me], sib_s.at[chips - 1], sib_r.at[chips - 1], sibling))
    for i in range(5):
        moves.append(send(edges_in[i], edges_out[i], pair_s.at[i], pair_r.at[i], pair))
    for j in range(chips - 1):
        direct[j].wait_recv()
        block = lax.rem(chip + chips - 1 - j, chips) * 2 + core
        moves.append(send(table.at[block], table.at[block], sib_s.at[j], sib_r.at[j], sibling))
    for copy in direct:
        copy.wait_send()
    for copy in moves:
        copy.wait()
    own.wait()


def split(x):
    high = x.astype(BF16)
    return high, (x - high.astype(F32)).astype(BF16)


def dot(left, right, dims=NN):
    return lax.dot_general(left, right, dims, preferred_element_type=F32)


def edge_kernel(
    shards, slot, counts, negatives, lhs_ids, rhs_ids, rel_ids, lhs_tab, rhs_tab, relation, drhs, dlhs, drel,
    oh_l, oh_r, oh_rel, lhs_s, rhs_s, lhs_b, rhs_b, glhs, grhs, live_col, live_row,
):
    width, rows = lhs_tab.shape
    rels = relation.shape[0]
    spans = lhs_s.shape[0]
    edges = spans * CH
    subs = edges // LANES
    per = CH // LANES
    runs, run_rows, run = oh_r.shape
    owners = run_rows // rows

    def onehot(number, count):
        ids = lax.broadcasted_iota(jnp.int32, (count, LANES), 0)
        return jnp.where(ids == number, 1.0, 0.0).astype(BF16)

    lane = lax.broadcasted_iota(jnp.int32, (1, LANES), 1)
    lhs_rows = lhs_ids[...].reshape(subs, LANES)
    rhs_rows = rhs_ids[...].reshape(subs, LANES)
    rel_rows = rel_ids[...].reshape(subs, LANES)
    for j in range(subs):
        at = slice((j % per) * LANES, (j % per + 1) * LANES)
        oh_l[j // per, :, at] = onehot(lhs_rows[j : j + 1, :], rows)
        oh_rel[j // per, :, at] = onehot(rel_rows[j : j + 1, :], rels)
        inside = (j * LANES) % run
        shift = jnp.zeros((1, LANES), jnp.int32)
        for g in range(1, owners):
            shift = shift + jnp.where(inside + lane >= g * slot, rows, 0)
        oh_r[(j * LANES) // run, :, inside : inside + LANES] = onehot(rhs_rows[j : j + 1, :] + shift, run_rows)
    for o in range(shards):
        steps = lax.broadcasted_iota(jnp.int32, (slot, 1), 0)
        live_col[o * slot : (o + 1) * slot, :] = jnp.where(steps < counts[0, o], 1.0, 0.0)
    for c in range(spans):
        place = c * CH + lax.broadcasted_iota(jnp.int32, (1, CH), 1)
        live = jnp.zeros((1, CH), F32)
        for o in range(c * CH // slot, min(shards, -(-(c + 1) * CH // slot))):
            here = (place >= o * slot) & (place < o * slot + counts[0, o])
            live = jnp.where(here, 1.0, live)
        live_row[c] = live

    lhs_high, lhs_low = split(lhs_tab[...])
    rel_high, rel_low = split(relation[...])
    for c in range(spans):
        high = dot(lhs_high, oh_l[c])
        lhs_s[c] = high + dot(lhs_low, oh_l[c])
        lhs_b[c] = high.astype(BF16)
    for t in range(runs):
        parts = [split(rhs_tab[t * owners + g]) for g in range(owners)]
        high = dot(jnp.concatenate([p[0] for p in parts], axis=1), oh_r[t])
        low = dot(jnp.concatenate([p[1] for p in parts], axis=1), oh_r[t])
        both, high = high + low, high.astype(BF16)
        for i in range(run // LANES):
            k = t * run // LANES + i
            at = slice((k % per) * LANES, (k % per + 1) * LANES)
            rhs_s[k // per, :, at] = both[:, i * LANES : (i + 1) * LANES]
            rhs_b[k // per, :, at] = high[:, i * LANES : (i + 1) * LANES]
    glhs[...] = jnp.zeros_like(glhs)
    grhs[...] = jnp.zeros_like(grhs)

    def soft(positive, scores, live):
        masked = jnp.where(live, scores, -jnp.inf)
        top = jnp.maximum(positive, jnp.max(masked, axis=0, keepdims=True))
        own = jnp.exp(positive - top)
        others = jnp.exp(masked - top)
        scale = 1.0 / (own + jnp.sum(others, axis=0, keepdims=True))
        return others, own * scale, scale

    rel_total = jnp.zeros((rels, width), F32)
    for c in range(spans):
        n = negatives[c]
        lhs, rhs = lhs_s[c], rhs_s[c]
        rel = dot(rel_high, oh_rel[c], TN) + dot(rel_low, oh_rel[c], TN)
        live = live_row[c]
        live_neg = live_col[pl.ds(pl.multiple_of(n * CH, CH), CH), :] > 0.5
        left, right = lhs * rel, rhs * rel
        positive = jnp.sum(left * rhs, axis=0, keepdims=True)
        left_b, right_b = left.astype(BF16), right.astype(BF16)
        rhs_neg, lhs_neg = rhs_b[n], lhs_b[n]
        tail, tail_pos, tail_scale = soft(positive, dot(rhs_neg, left_b, TN), live_neg)
        head, head_pos, head_scale = soft(positive, dot(lhs_neg, right_b, TN), live_neg)
        weight = live * (tail_pos + head_pos - 2.0)
        tail_w = (tail * (live * tail_scale)).astype(BF16)
        head_w = (head * (live * head_scale)).astype(BF16)
        grad_left = weight * rhs + dot(rhs_neg, tail_w)
        grad_right = dot(lhs_neg, head_w)
        glhs[c] += grad_left * rel
        grhs[c] += weight * left + grad_right * rel
        high, low = split(grad_left * lhs + grad_right * rhs)
        rel_total = rel_total + dot(oh_rel[c], high, NT) + dot(oh_rel[c], low, NT)
        grhs[n] += dot(left_b, tail_w, NT)
        glhs[n] += dot(right_b, head_w, NT)
    drel[...] = rel_total

    total = jnp.zeros((width, rows), F32)
    for c in range(spans):
        high, low = split(glhs[c])
        total = total + dot(high, oh_l[c], NT) + dot(low, oh_l[c], NT)
    dlhs[...] = total
    for t in range(runs):
        pieces = []
        for i in range(run // LANES):
            k = t * run // LANES + i
            pieces.append(grhs[k // per, :, (k % per) * LANES : (k % per + 1) * LANES])
        high, low = split(jnp.concatenate(pieces, axis=1))
        sums = dot(high, oh_r[t], NT) + dot(low, oh_r[t], NT)
        for g in range(owners):
            drhs[t * owners + g] = sums[:, g * rows : (g + 1) * rows]


def return_kernel(
    mask, doms, shards, drhs, dlhs, drel, accumulator, entity, state, rel_out,
    sib_land, sums, land, pair_land, rel_half, rel_sib, rel_sum, rel_chip, rel_sum2, rel_dom, rel_full, rel_back,
    pair_s, pair_r, sib_s, sib_r, chip_s, chip_r, rsib_s, rsib_r, rchip_s, rchip_r, rdom_s, rdom_r, rback_s, rback_r,
):
    chips = shards // 2
    half = rel_half.shape[0]
    dom, me = lax.axis_index("dom"), lax.axis_index("shard")
    chip, core = me // 2, lax.rem(me, 2)
    sibling = {"shard": chip * 2 + 1 - core}
    pair = {"dom": flip(dom, mask)}
    others = [{"shard": lax.rem(chip + j, chips) * 2 + core} for j in range(1, chips)]
    columns = [{"dom": lax.rem(dom + j, doms)} for j in range(1, doms)]
    greet([sibling] + columns + others)

    mine = pl.ds(pl.multiple_of(core * half, half), half)
    yours = pl.ds(pl.multiple_of((1 - core) * half, half), half)
    rel_half[...] = drel[yours, :]
    moves = [send(rel_half, rel_sib, rsib_s, rsib_r, sibling)]
    siblings = []
    for j in range(chips):
        place = lax.rem(chip + (j + 1) % chips, chips) * 2
        siblings.append(send(drhs.at[place + 1 - core], sib_land.at[j], sib_s.at[j], sib_r.at[j], sibling))
    home = send(dlhs, pair_land, pair_s, pair_r, pair)
    moves[0].wait_recv()
    rel_sum[...] = drel[mine, :] + rel_sib[...]
    rel_moves = [send(rel_sum, rel_chip.at[j], rchip_s.at[j], rchip_r.at[j], others[j]) for j in range(chips - 1)]
    directs = []
    for j in range(chips):
        place = lax.rem(chip + (j + 1) % chips, chips) * 2
        siblings[j].wait_recv()
        sums[j] = drhs[place + core] + sib_land[j]
        if j < chips - 1:
            directs.append(send(sums.at[j], land.at[j], chip_s.at[j], chip_r.at[j], others[j]))
    total = rel_sum[...]
    for j in range(chips - 1):
        rel_moves[j].wait_recv()
        total = total + rel_chip[j]
    rel_sum2[...] = total
    dom_moves = [send(rel_sum2, rel_dom.at[j], rdom_s.at[j], rdom_r.at[j], columns[j]) for j in range(doms - 1)]
    total = rel_sum2[...]
    for j in range(doms - 1):
        dom_moves[j].wait_recv()
    total = jnp.zeros_like(total)
    for d in range(doms):
        j = lax.rem(dom + doms - d, doms)
        total = total + jnp.where(j == 0, rel_sum2[...], rel_dom[jnp.maximum(j - 1, 0)])
    rel_full[...] = total
    back = send(rel_full, rel_back, rback_s, rback_r, sibling)
    grads = sums[chips - 1]
    for j in range(chips - 1):
        directs[j].wait_recv()
        grads = grads + land[j]
    home.wait_recv()
    grads = grads + pair_land[...]
    entity[...] = grads
    state[...] = accumulator[...] + jnp.sum(grads * grads, axis=0, keepdims=True) / grads.shape[0]
    back.wait_recv()
    rel_out[mine, :] = total
    rel_out[yours, :] = rel_back[...]
    for copy in moves + siblings + [home, back] + rel_moves + directs + dom_moves:
        copy.wait_send()


def local(doms, shards, embedding, accumulator, relation, plan, lhs_index, rhs_index, rel_index, slot_count, neg_span):
    rows, width = embedding.shape
    rels = relation.shape[0]
    edges = lhs_index.shape[0]
    slot = edges // shards
    chips = shards // 2
    spans = edges // CH
    run = math.lcm(slot, LANES)
    runs, owners = edges // run, run // slot
    half = rels // 2
    flips = doms - 1
    any_space = pl.BlockSpec(memory_space=pl.ANY)
    vmem = pl.BlockSpec(memory_space=pltpu.VMEM)
    smem = pl.BlockSpec(memory_space=pltpu.SMEM)
    dma = pltpu.SemaphoreType.DMA
    block = jax.ShapeDtypeStruct((width, rows), F32)
    table_type = jax.ShapeDtypeStruct((shards, width, rows), F32)
    branch = jnp.clip(plan[0] - 1, 0, flips - 1)
    edge_args = (lhs_index, rhs_index, rel_index, slot_count, neg_span)

    def fetch(mask, emb, *edge_args):
        return pl.pallas_call(
            functools.partial(fetch_kernel, mask, shards),
            out_shape=(block,) + tuple(jax.ShapeDtypeStruct(x.shape, x.dtype) for x in edge_args) + (table_type,),
            in_specs=[any_space] * 6,
            out_specs=(any_space,) * 7,
            scratch_shapes=[
                dma, dma((6,)), dma((6,)), dma((chips - 1,)), dma((chips - 1,)), dma((chips,)), dma((chips,)),
            ],
            compiler_params=pltpu.CompilerParams(collective_id=mask - 1, has_side_effects=True),
            name="fetch_rows",
        )(emb, *edge_args)

    lhs_tab, lhs_ids, rhs_ids, rel_ids, counts, negatives, table = lax.switch(
        branch, [functools.partial(fetch, mask) for mask in range(1, doms)], embedding.T, *edge_args
    )

    drhs, dlhs, drel = pl.pallas_call(
        functools.partial(edge_kernel, shards, slot),
        out_shape=(table_type, block, jax.ShapeDtypeStruct((rels, width), F32)),
        in_specs=[smem] * 2 + [vmem] * 6,
        out_specs=(vmem,) * 3,
        scratch_shapes=[
            pltpu.VMEM((spans, rows, CH), BF16),
            pltpu.VMEM((runs, owners * rows, run), BF16),
            pltpu.VMEM((spans, rels, CH), BF16),
            pltpu.VMEM((spans, width, CH), F32),
            pltpu.VMEM((spans, width, CH), F32),
            pltpu.VMEM((spans, width, CH), BF16),
            pltpu.VMEM((spans, width, CH), BF16),
            pltpu.VMEM((spans, width, CH), F32),
            pltpu.VMEM((spans, width, CH), F32),
            pltpu.VMEM((edges, 1), F32),
            pltpu.VMEM((spans, 1, CH), F32),
        ],
        compiler_params=pltpu.CompilerParams(vmem_limit_bytes=56 * 1024 * 1024),
        name="edge_grads",
    )(counts, negatives, lhs_ids, rhs_ids, rel_ids, lhs_tab, table, relation)

    def give_back(mask, drhs, dlhs, drel, acc):
        small = pltpu.VMEM((half, width), F32)
        return pl.pallas_call(
            functools.partial(return_kernel, mask, doms, shards),
            out_shape=(
                block,
                jax.ShapeDtypeStruct((1, rows), F32),
                jax.ShapeDtypeStruct((rels, width), F32),
            ),
            in_specs=[vmem] * 4,
            out_specs=(vmem,) * 3,
            scratch_shapes=[
                pltpu.VMEM((chips, width, rows), F32),
                pltpu.VMEM((chips, width, rows), F32),
                pltpu.VMEM((chips - 1, width, rows), F32),
                pltpu.VMEM((width, rows), F32),
                small, small, small,
                pltpu.VMEM((chips - 1, half, width), F32),
                small,
                pltpu.VMEM((doms - 1, half, width), F32),
                small, small,
                dma, dma, dma((chips,)), dma((chips,)), dma((chips - 1,)), dma((chips - 1,)),
                dma, dma, dma((chips - 1,)), dma((chips - 1,)), dma((doms - 1,)), dma((doms - 1,)), dma, dma,
            ],
            compiler_params=pltpu.CompilerParams(
                collective_id=flips + mask - 1, has_side_effects=True, vmem_limit_bytes=56 * 1024 * 1024
            ),
            name="return_grads",
        )(drhs, dlhs, drel, acc)

    entity, state, rel_grad = lax.switch(
        branch,
        [functools.partial(give_back, mask) for mask in range(1, doms)],
        drhs, dlhs, drel, accumulator.reshape(1, rows),
    )
    return entity.T, state.reshape(rows), rel_grad


def solution(mesh):
    both = ("dom", "shard")
    in_specs = (P(both, None), P(both), P(), P(), P(both), P(both), P(both), P(both, None), P(both))
    out_specs = (P(both, None), P(both), P())
    body = functools.partial(local, mesh.shape["dom"], mesh.shape["shard"])
    return jax.shard_map(body, mesh=mesh, in_specs=in_specs, out_specs=out_specs, check_vma=False)
```
